32 devices in a mesh: dir: 4 (over x, core), bond: 8 (over z, y).
Axes of the slice: x: 2, y: 2, z: 4, core: 2. Of those that a mesh axis runs over, the one named last changes fastest.
Arguments:
- corner_mat: bfloat16 [4, 8192, 8192], P('dir', 'bond'), may hold values from -0.0625 to 0.0625
- edge_mat: bfloat16 [4, 32768, 8192], P('dir', 'bond'), may hold values from -0.0625 to 0.0625
- edge_panel: bfloat16 [4, 8192, 512], P('dir', 'bond'), may hold values from -6 to 6
- vertex_weights: float32 [4, 4, 4], replicated, may hold values from -3 to 3
- projector: bfloat16 [4, 512, 256], P('dir'), may hold values from -0.25 to 0.25
- edge_projector: bfloat16 [4, 8192, 256], P('dir', 'bond'), may hold values from -0.09375 to 0.09375
Outputs:
- new_corner: bfloat16 [4, 32768, 256], P('dir', 'bond')
- gram: float32 [4, 256, 256], P('dir', 'bond')
- new_edge: bfloat16 [4, 256, 512], P('dir', 'bond')
The draws below stay inside these ranges and needn't reach their ends.
All inputs are finite; a program needn't handle non-finite values.
Results may differ from the reference program's by a relative error of at most 0.0065.
Values may be sent and summed in bfloat16 or wider, within the bound.
A program may use at most 256 MiB of HBM per device.

```python
import jax
import jax.numpy as jnp
from jax import lax

CHI = 8192
D = 4
PANEL = 512
KEEP = 256


def with_spikes(array, key, source, target, blocks, factor):
    owner, partner = [(jnp.arange(array.shape[axis_at]) // (array.shape[axis_at] // blocks)).reshape([-1 if axis == axis_at else 1 for axis in range(array.ndim)]) for axis_at in (source, target)]
    chosen = jax.random.permutation(key, blocks)[partner]
    strong = (owner == chosen) | (owner == (partner + blocks // 2) % blocks)
    return jnp.where(strong, factor * array, array)


def steps_of(key, dims, cuts, least, top_value):
    def one(axis_at, shards_of):
        heights = jax.random.uniform(jax.random.fold_in(jax.random.fold_in(key, 6), axis_at), (shards_of,), jnp.float32, least / len(cuts), top_value / len(cuts))
        return jnp.repeat(jnp.exp(heights), dims[axis_at] // shards_of).reshape((-1,) + (1,) * (len(dims) - axis_at - 1))

    level = one(*cuts[0])
    for cut in cuts[1:]:
        level = level * one(*cut)
    return level


def bell_draw(key, shape, scale, reach, cuts=(), held_as=jnp.bfloat16):
    values = jax.random.normal(key, shape, jnp.float32) * scale
    if len(cuts) > 0:
        values = steps_of(key, shape, cuts, -0.22, 0.18) * values
    return jnp.clip(values, min=-reach, max=reach).astype(held_as)


def bell_draw_with(key, extent, scale, most, split, heavy, held_as=jnp.bfloat16):
    result = scale * jax.random.normal(key, extent, jnp.float32)
    if split:
        result = result * steps_of(key, extent, split, -0.22, 0.18)
    return jnp.clip(with_spikes(result, jax.random.fold_in(key, 3), *heavy), -most, most).astype(held_as)


def setup_inputs(seed: int = 0) -> dict:
    seeds = jax.random.split(jax.random.key(seed), 7)
    return {
        "corner_mat": bell_draw(seeds[0], (4, CHI, CHI), CHI ** -0.5, 0.0625, ((0, 4), (1, 8))),
        "edge_mat": bell_draw(seeds[1], (4, CHI * D, CHI), CHI ** -0.5, 0.0625, ((0, 4), (1, 8))),
        "edge_panel": bell_draw(seeds[2], (4, CHI, PANEL), 1.0, 6.0, ((0, 4), (1, 8))),
        "vertex_weights": bell_draw(seeds[3], (D, D, D), D ** -0.5, 3.0, (), jnp.float32),
        "projector": bell_draw(seeds[4], (4, PANEL, KEEP), PANEL ** -0.5, 0.25, ((0, 4),)),
        "edge_projector": bell_draw_with(seeds[5], (4, CHI, KEEP), CHI ** -0.5, 0.09375, ((0, 4), (1, 8)), (1, 2, 8, 2.0)),
    }


def enlarge(previous, hidden_panel, vertex_weights):
    raw_block = jnp.dot(previous, hidden_panel, preferred_element_type=jnp.float32)
    row_count = raw_block.shape[0] // D
    split_block = raw_block.reshape(row_count, D, D, PANEL // D)
    mixed_block = jnp.einsum("isub,sut->istb", split_block, vertex_weights, precision=lax.Precision.HIGHEST)
    return mixed_block.reshape(row_count * D, PANEL).astype(jnp.bfloat16)


def reference(corner_mat, edge_mat, edge_panel, vertex_weights, projector, edge_projector):
    corners_out = []
    grams_out = []
    edges_out = []
    for direction in range(4):
        hidden_panel = jnp.dot(corner_mat[direction], edge_panel[direction], preferred_element_type=jnp.float32).astype(jnp.bfloat16)
        enlarged = enlarge(edge_mat[(direction - 1) % 4], hidden_panel, vertex_weights)
        projected = jnp.dot(enlarged, projector[direction], preferred_element_type=jnp.float32)
        corners_out.append(projected.astype(jnp.bfloat16))
        grams_out.append(jnp.dot(projected.T, projected, precision=lax.Precision.HIGHEST) / (CHI * D))
        edges_out.append(jnp.dot(edge_projector[direction].T, edge_panel[direction], preferred_element_type=jnp.float32).astype(jnp.bfloat16))
    return jnp.stack(corners_out), jnp.stack(grams_out), jnp.stack(edges_out)
```

```python
import jax
import jax.numpy as jnp
from jax import lax
from jax.sharding import PartitionSpec as P

D = 4


def to_lower(block):
    n = lax.axis_size("dir")
    return lax.ppermute(block, "dir", [(i, (i - 1) % n) for i in range(n)])


def to_upper(block):
    n = lax.axis_size("dir")
    return lax.ppermute(block, "dir", [(i, (i + 1) % n) for i in range(n)])


def on_device(corner_mat, edge_mat, edge_panel, vertex_weights, projector, edge_projector):
    corner_rows = corner_mat[0]
    own_edge = edge_mat[0]
    panel_rows = edge_panel[0]
    n_dir = lax.axis_size("dir")
    rows, panel = own_edge.shape[0], panel_rows.shape[1]
    chi = own_edge.shape[1]
    gathered = lax.all_gather(panel_rows, "bond", axis=0, tiled=True)
    hidden = jnp.dot(corner_rows, gathered, preferred_element_type=jnp.float32).astype(jnp.bfloat16)
    new_edge = lax.psum_scatter(
        jnp.dot(edge_projector[0].T, panel_rows, preferred_element_type=jnp.float32),
        "bond", scatter_dimension=0, tiled=True,
    ).astype(jnp.bfloat16)
    upper_hidden = lax.all_gather(to_lower(hidden), "bond", axis=0, tiled=True)
    upper_proj = to_lower(projector[0])
    raw = jnp.dot(own_edge, upper_hidden, preferred_element_type=jnp.float32)
    coef = jnp.tile(vertex_weights, (rows // D, 1, 1))
    parts = [raw[:, u * (panel // D):(u + 1) * (panel // D)] for u in range(D)]
    mixed = [
        sum(coef[:, u, t][:, None] * parts[u] for u in range(D)) for t in range(D)
    ]
    enlarged = jnp.concatenate(mixed, axis=1).astype(jnp.bfloat16)
    projected = jnp.dot(enlarged, upper_proj, preferred_element_type=jnp.float32)
    new_corner = to_upper(projected.astype(jnp.bfloat16))
    high = projected.astype(jnp.bfloat16)
    low = (projected - high.astype(jnp.float32)).astype(jnp.bfloat16)
    cross = jnp.dot(high.T, low, preferred_element_type=jnp.float32)
    partial = jnp.dot(high.T, high, preferred_element_type=jnp.float32) + cross + cross.T
    gram = to_upper(lax.psum_scatter(partial, "bond", scatter_dimension=0, tiled=True)) / (chi * D)
    return (new_corner[None], gram[None], new_edge[None])


def solution(mesh):
    in_specs = (
        P("dir", "bond", None),
        P("dir", "bond", None),
        P("dir", "bond", None),
        P(),
        P("dir", None, None),
        P("dir", "bond", None),
    )
    out_specs = (P("dir", "bond", None), P("dir", "bond", None), P("dir", "bond", None))
    return jax.shard_map(
        on_device, mesh=mesh, in_specs=in_specs, out_specs=out_specs, check_vma=False
    )
```

```python
import functools

import jax
import jax.numpy as jnp
from jax import lax
from jax.experimental import pallas as pl
from jax.experimental.pallas import tpu as pltpu
from jax.sharding import PartitionSpec as P

D = 4
PIECES = 2
DEPTH = 3
TILE = 512
MESH = pl.DeviceIdType.MESH
F32 = jnp.float32
BF16 = jnp.bfloat16


def over_rows(left, right):
    return lax.dot_general(left, right, (((0,), (0,)), ((), ())), preferred_element_type=F32)


def fused_kernel(
    n, n_dir,
    c_ref, a_ref, e_ref, f_ref, p_ref, w_ref,
    corner_out, gram_out, edge_out,
    e_all, h_all, raw_sum, hid_sum, hid, a_buf, c_buf, out_buf, p_up,
    edge_part, edge_recv, gram_high, gram_cross, gram_part, gram_recv,
    e_send, e_recv, h_send, h_recv, c_sem, a_sem, hid_send, hid_recv,
    p_send, p_recv, out_send, out_recv, es_send, es_recv, g_send, g_recv, go,
):
    k = lax.axis_index("dir")
    b = lax.axis_index("bond")
    up, down = lax.rem(k + 1, n_dir), lax.rem(k + n_dir - 1, n_dir)
    odd_dir = lax.rem(k, 2)
    odd = lax.rem(b, 2)
    pos = (1 - odd) * (b // 2) + odd * (n - 1 - b // 2)

    def bond_at(place):
        place = lax.rem(place, n)
        back = place // (n // 2)
        return (1 - back) * (2 * place) + back * (2 * (n - 1 - place) + 1)

    right, left = bond_at(pos + 1), bond_at(pos + n - 1)
    rows = e_ref.shape[0]
    half = rows // 2
    piece = half // PIECES
    total_rows = a_ref.shape[0]
    chunks = 2 * n

    barrier = pltpu.get_barrier_semaphore()
    for j in range(n):
        if j > 0:
            pl.semaphore_signal(barrier, inc=1, device_id=(k, lax.rem(b + j, n)), device_id_type=MESH)
        pl.semaphore_signal(barrier, inc=1, device_id=(up, lax.rem(b + j, n)), device_id_type=MESH)
        pl.semaphore_signal(barrier, inc=1, device_id=(down, lax.rem(b + j, n)), device_id_type=MESH)

    def columns(j):
        way, hops = lax.rem(j, 2), j // 2
        owner = bond_at(pos + (1 - way) * (n - hops) + way * hops)
        return pl.ds(pl.multiple_of(owner * rows + way * half, half), half)

    def c_load(j):
        return pltpu.make_async_copy(c_ref.at[:, columns(j)], c_buf.at[lax.rem(j, DEPTH)], c_sem.at[lax.rem(j, DEPTH)])

    def a_load(j):
        return pltpu.make_async_copy(a_ref.at[:, columns(j)], a_buf.at[lax.rem(j, DEPTH)], a_sem.at[lax.rem(j, DEPTH)])

    for j in range(DEPTH - 1):
        c_load(j).start()
        a_load(j).start()

    e_all[0, 0] = e_ref[:half]
    e_all[1, 0] = e_ref[half:]

    def hop(panels, sends, recvs, way, slot, q):
        part = pl.ds(q * piece, piece)
        return pltpu.make_async_remote_copy(
            src_ref=panels.at[way, slot, part],
            dst_ref=panels.at[way, slot + 1, part],
            send_sem=sends.at[way, slot, q],
            recv_sem=recvs.at[way, slot, q],
            device_id=(k, left if way else right),
            device_id_type=MESH,
        )

    def start_ring(panels, sends, recvs):
        for q in range(PIECES):
            for way in range(2):
                hop(panels, sends, recvs, way, 0, q).start()

    def run_ring(panels, sends, recvs, add, gate):
        add(0, True)

        @pl.loop(1, n)
        def _(s):
            for q in range(PIECES):
                for way in range(2):
                    hop(panels, sends, recvs, way, s - 1, q).wait_recv()

                    @pl.when(s < n - 1)
                    def _():
                        hop(panels, sends, recvs, way, s, q).start()

                if q == PIECES - 1:
                    @pl.when(s == n - 2)
                    def _():
                        gate()
                add(2 * s - 1 + q, False)

    def end_ring(panels, sends, recvs):
        @pl.loop(0, n - 1)
        def _(s):
            for q in range(PIECES):
                for way in range(2):
                    hop(panels, sends, recvs, way, s, q).wait_send()

    def prefetch(load, j):
        @pl.when(j + DEPTH - 1 < chunks)
        def _():
            load(j + DEPTH - 1).start()

    def add_hidden(j, first):
        prefetch(c_load, j)
        c_load(j).wait()
        slot = lax.rem(j, DEPTH)
        way, hops = lax.rem(j, 2), j // 2

        @pl.loop(0, rows // TILE)
        def _(r):
            span = pl.ds(pl.multiple_of(r * TILE, TILE), TILE)
            term = jnp.dot(c_buf[slot, span, :], e_all[way, hops], preferred_element_type=F32)
            hid_sum[span, :] = term if first else hid_sum[span, :] + term

    def add_raw(j, first):
        prefetch(a_load, j)
        a_load(j).wait()
        slot = lax.rem(j, DEPTH)
        way, hops = lax.rem(j, 2), j // 2

        @pl.loop(0, total_rows // TILE)
        def _(r):
            span = pl.ds(pl.multiple_of(r * TILE, TILE), TILE)
            term = jnp.dot(a_buf[slot, span, :], h_all[way, hops], preferred_element_type=F32)
            raw_sum[span, :] = term if first else raw_sum[span, :] + term

    pl.semaphore_wait(barrier, 3 * n - 1)

    p_copy = pltpu.make_async_remote_copy(
        src_ref=p_ref, dst_ref=p_up, send_sem=p_send, recv_sem=p_recv,
        device_id=(down, b), device_id_type=MESH,
    )

    def edge_copy(j):
        target = lax.rem(b + j, n)
        return pltpu.make_async_remote_copy(
            src_ref=edge_part.at[target], dst_ref=edge_recv.at[j],
            send_sem=es_send.at[j], recv_sem=es_recv.at[j],
            device_id=(k, target), device_id_type=MESH,
        )

    @pl.when(odd_dir == 1)
    def _():
        pl.semaphore_wait(go, 1)

    start_ring(e_all, e_send, e_recv)
    p_copy.start()

    slab = edge_part.shape[1]
    keep = f_ref.shape[1]
    edge_sum = over_rows(f_ref[...], e_ref[...])
    for r in range(n):
        edge_part[r] = edge_sum[r * slab:(r + 1) * slab]
    for j in range(1, n):
        edge_copy(j).start()

    def open_odd():
        @pl.when(odd_dir == 0)
        def _():
            pl.semaphore_signal(go, inc=1, device_id=(up, b), device_id_type=MESH)

    def open_even():
        @pl.when(odd_dir == 1)
        def _():
            pl.semaphore_signal(go, inc=1, device_id=(down, b), device_id_type=MESH)

    run_ring(e_all, e_send, e_recv, add_hidden, open_odd)
    add_hidden(chunks - 1, False)
    hid[...] = hid_sum[...].astype(BF16)

    def hid_copy(way):
        return pltpu.make_async_remote_copy(
            src_ref=hid.at[pl.ds(way * half, half)], dst_ref=h_all.at[way, 0],
            send_sem=hid_send.at[way], recv_sem=hid_recv.at[way],
            device_id=(down, b), device_id_type=MESH,
        )

    for way in range(2):
        hid_copy(way).start()
    end_ring(e_all, e_send, e_recv)

    for j in range(1, n):
        edge_copy(j).wait()
    edge_total = edge_part[b]
    for j in range(1, n):
        edge_total = edge_total + edge_recv[j]
    edge_out[...] = edge_total.astype(BF16)

    for way in range(2):
        hid_copy(way).wait()

    @pl.when(odd_dir == 0)
    def _():
        pl.semaphore_wait(go, 1)

    start_ring(h_all, h_send, h_recv)
    run_ring(h_all, h_send, h_recv, add_raw, open_even)

    p_copy.wait()
    last = chunks - 1
    a_load(last).wait()
    gram_high[...] = jnp.zeros_like(gram_high)
    gram_cross[...] = jnp.zeros_like(gram_cross)
    width = e_ref.shape[1] // D

    def out_copy(r):
        span = pl.ds(pl.multiple_of(r * TILE, TILE), TILE)
        return pltpu.make_async_remote_copy(
            src_ref=out_buf.at[span], dst_ref=corner_out.at[span],
            send_sem=out_send.at[r], recv_sem=out_recv.at[r],
            device_id=(up, b), device_id_type=MESH,
        )

    @pl.loop(0, total_rows // TILE)
    def _(r):
        span = pl.ds(pl.multiple_of(r * TILE, TILE), TILE)
        raw = raw_sum[span, :] + jnp.dot(
            a_buf[last % DEPTH, span, :], h_all[1, n - 1], preferred_element_type=F32
        )
        parts = [raw[:, u * width:(u + 1) * width].reshape(TILE // 8, 8, width) for u in range(D)]
        mixed = []
        for t in range(D):
            total = parts[0] * w_ref[t][None]
            for u in range(1, D):
                total = total + parts[u] * w_ref[u * D + t][None]
            mixed.append(total.reshape(TILE, width).astype(BF16))
        projected = jnp.dot(jnp.concatenate(mixed, axis=1), p_up[...], preferred_element_type=F32)
        high = projected.astype(BF16)
        out_buf[span, :] = high
        out_copy(r).start()
        low = (projected - high.astype(F32)).astype(BF16)
        gram_high[...] += over_rows(high, high)
        gram_cross[...] += over_rows(high, low)

    gram_sum = gram_high[...] + (gram_cross[...] + gram_cross[...].T)
    g_slab = gram_part.shape[1]
    for r in range(n):
        gram_part[r] = gram_sum[r * g_slab:(r + 1) * g_slab]

    def gram_copy(j):
        target = lax.rem(b + j, n)
        return pltpu.make_async_remote_copy(
            src_ref=gram_part.at[target], dst_ref=gram_recv.at[j],
            send_sem=g_send.at[j], recv_sem=g_recv.at[j],
            device_id=(up, target), device_id_type=MESH,
        )

    for j in range(n):
        gram_copy(j).start()
    end_ring(h_all, h_send, h_recv)
    for j in range(n):
        gram_copy(j).wait()
    gram_total = gram_recv[0]
    for j in range(1, n):
        gram_total = gram_total + gram_recv[j]
    gram_out[...] = gram_total / (c_ref.shape[1] * D)

    @pl.loop(0, total_rows // TILE)
    def _(r):
        out_copy(r).wait()


def in_one_kernel(n, n_dir, corner_mat, edge_mat, edge_panel, vertex_weights, projector, edge_projector):
    rows, panel = edge_panel.shape[1:]
    total_rows = edge_mat.shape[1]
    keep = projector.shape[2]
    width = panel // D
    half = rows // 2
    piece_shape = (2, n - 1, PIECES)
    tiles = total_rows // TILE
    coef = jnp.broadcast_to(
        jnp.tile(vertex_weights.transpose(1, 2, 0).reshape(D * D, D), (1, 8 // D))[:, :, None], (D * D, 8, width)
    )
    vmem = pl.BlockSpec(memory_space=pltpu.VMEM)
    anywhere = pl.BlockSpec(memory_space=pl.ANY)
    dma = pltpu.SemaphoreType.DMA
    flops = 2 * panel * corner_mat.shape[2] * (rows + total_rows)
    corner, gram, edge = pl.pallas_call(
        functools.partial(fused_kernel, n, n_dir),
        out_shape=(
            jax.ShapeDtypeStruct((total_rows, keep), BF16),
            jax.ShapeDtypeStruct((keep // n, keep), F32),
            jax.ShapeDtypeStruct((keep // n, panel), BF16),
        ),
        in_specs=[anywhere, anywhere, vmem, vmem, vmem, vmem],
        out_specs=(anywhere, vmem, vmem),
        scratch_shapes=[
            pltpu.VMEM((2, n, half, panel), BF16),
            pltpu.VMEM((2, n, half, panel), BF16),
            pltpu.VMEM((total_rows, panel), F32),
            pltpu.VMEM((rows, panel), F32),
            pltpu.VMEM((rows, panel), BF16),
            pltpu.VMEM((DEPTH, total_rows, half), BF16),
            pltpu.VMEM((DEPTH, rows, half), BF16),
            pltpu.VMEM((total_rows, keep), BF16),
            pltpu.VMEM((panel, keep), BF16),
            pltpu.VMEM((n, keep // n, panel), F32),
            pltpu.VMEM((n, keep // n, panel), F32),
            pltpu.VMEM((keep, keep), F32),
            pltpu.VMEM((keep, keep), F32),
            pltpu.VMEM((n, keep // n, keep), F32),
            pltpu.VMEM((n, keep // n, keep), F32),
            dma(piece_shape), dma(piece_shape), dma(piece_shape), dma(piece_shape),
            dma((DEPTH,)), dma((DEPTH,)), dma((2,)), dma((2,)),
            dma, dma, dma((tiles,)), dma((tiles,)),
            dma((n,)), dma((n,)), dma((n,)), dma((n,)),
            pltpu.SemaphoreType.REGULAR,
        ],
        compiler_params=pltpu.CompilerParams(
            collective_id=0, has_side_effects=True, vmem_limit_bytes=60 * 1024 * 1024
        ),
        cost_estimate=pl.CostEstimate(
            flops=flops, bytes_accessed=2 * corner_mat.shape[2] * (rows + total_rows), transcendentals=0
        ),
        name="corner_window",
    )(corner_mat[0], edge_mat[0], edge_panel[0], edge_projector[0], projector[0], coef)
    return (corner[None], gram[None], edge[None])


def to_lower(block):
    n = lax.axis_size("dir")
    return lax.ppermute(block, "dir", [(i, (i - 1) % n) for i in range(n)])


def to_upper(block):
    n = lax.axis_size("dir")
    return lax.ppermute(block, "dir", [(i, (i + 1) % n) for i in range(n)])


def in_many_ops(corner_mat, edge_mat, edge_panel, vertex_weights, projector, edge_projector):
    corner_rows = corner_mat[0]
    own_edge = edge_mat[0]
    panel_rows = edge_panel[0]
    n_dir = lax.axis_size("dir")
    rows, panel = own_edge.shape[0], panel_rows.shape[1]
    chi = own_edge.shape[1]
    gathered = lax.all_gather(panel_rows, "bond", axis=0, tiled=True)
    hidden = jnp.dot(corner_rows, gathered, preferred_element_type=jnp.float32).astype(jnp.bfloat16)
    new_edge = lax.psum_scatter(
        jnp.dot(edge_projector[0].T, panel_rows, preferred_element_type=jnp.float32),
        "bond", scatter_dimension=0, tiled=True,
    ).astype(jnp.bfloat16)
    upper_hidden = lax.all_gather(to_lower(hidden), "bond", axis=0, tiled=True)
    upper_proj = to_lower(projector[0])
    raw = jnp.dot(own_edge, upper_hidden, preferred_element_type=jnp.float32)
    coef = jnp.tile(vertex_weights, (rows // D, 1, 1))
    parts = [raw[:, u * (panel // D):(u + 1) * (panel // D)] for u in range(D)]
    mixed = [
        sum(coef[:, u, t][:, None] * parts[u] for u in range(D)) for t in range(D)
    ]
    enlarged = jnp.concatenate(mixed, axis=1).astype(jnp.bfloat16)
    projected = jnp.dot(enlarged, upper_proj, preferred_element_type=jnp.float32)
    new_corner = to_upper(projected.astype(jnp.bfloat16))
    high = projected.astype(jnp.bfloat16)
    low = (projected - high.astype(jnp.float32)).astype(jnp.bfloat16)
    cross = jnp.dot(high.T, low, preferred_element_type=jnp.float32)
    partial = jnp.dot(high.T, high, preferred_element_type=jnp.float32) + cross + cross.T
    gram = to_upper(lax.psum_scatter(partial, "bond", scatter_dimension=0, tiled=True)) / (chi * D)
    return (new_corner[None], gram[None], new_edge[None])


def solution(mesh):
    n, n_dir = mesh.shape["bond"], mesh.shape["dir"]
    small = n % 2 == 0 and n_dir % 2 == 0 and n_dir > 2 and n <= 8
    on_device = functools.partial(in_one_kernel, n, n_dir) if small else in_many_ops
    in_specs = (
        P("dir", "bond", None),
        P("dir", "bond", None),
        P("dir", "bond", None),
        P(),
        P("dir", None, None),
        P("dir", "bond", None),
    )
    out_specs = (P("dir", "bond", None), P("dir", "bond", None), P("dir", "bond", None))
    return jax.shard_map(
        on_device, mesh=mesh, in_specs=in_specs, out_specs=out_specs, check_vma=False
    )
```
